32 devices in a mesh: groups: 2 (over y), gx: 8 (over z, x), gy: 2 (over core).
Axes of the slice: x: 2, y: 2, z: 4, core: 2. Of those that a mesh axis runs over, the one named last changes fastest.
Arguments:
- activations: bfloat16 [2, 256, 4096], P('gy', 'groups', 'gx'), parts along dimension 1, may hold values from -6 to 6
- gate_tiles: bfloat16 [256, 40, 128, 128], P('gx', 'gy'), may hold values from -0.09375 to 0.09375
- up_tiles: bfloat16 [256, 40, 128, 128], P('gx', 'gy'), may hold values from -0.09375 to 0.09375
- down_tiles: bfloat16 [256, 40, 128, 128], P('gx', 'gy'), may hold values from -0.046875 to 0.046875
- gate_slots: int32 [256, 40], P('gx', 'gy'), may hold values from -1 to 31, as said below
- up_slots: int32 [256, 40], P('gx', 'gy'), may hold values from -1 to 31, as said below
- down_slots: int32 [256, 40], P('gx', 'gy'), may hold values from -1 to 31, as said below
Outputs:
- mixed_out: bfloat16 [2, 256, 4096], P('gy', 'groups', 'gx'), parts along dimension 1
The draws below stay inside these ranges and needn't reach their ends.
There are 2 independent parts, one for each index of `groups`. The reference program is written for one: setup_inputs(seed, part) draws one part's arguments, and reference() takes and returns one part's arrays. A program takes and returns all parts, laid end to end along the dimension named above; an argument that names none is the same for every part. Nothing has to cross between parts.
Inputs may be any that keep to these rules, and one draw needn't show every extreme that they name: `gate_slots`: in each block column and each half of the model width (the 20 slots of one half), the entries that are not -1 come first, are distinct, and number between 12 and 20; some list holds exactly 20. `up_slots`: as for gate_slots. `down_slots`: as for gate_slots.
All inputs are finite; a program needn't handle non-finite values.
Results may differ from the reference program's by a relative error of at most 0.005.
Values may be sent and summed in bfloat16 or wider, within the bound.
A program may use at most 256 MiB of HBM per device.

```python
import jax
import jax.numpy as jnp
from jax import lax

D = 8192
FF = 32768
BLK = 128
CAP = 20
TOKENS = 128
N_GY = 2


def slot_lists(key):
    list_total = FF // BLK * N_GY
    half_blocks = D // BLK // N_GY
    list_keys = jax.random.split(key, list_total)
    orders = jax.vmap(lambda single: jax.random.permutation(single, half_blocks))(list_keys)[:, :CAP]
    lowest = 3 * CAP // 5
    live_counts = jax.random.randint(jax.random.fold_in(key, 1), (list_total,), lowest, CAP + 1)
    full_list = jax.random.randint(jax.random.fold_in(key, 2), (), 0, list_total)
    live_counts = jnp.where(jnp.arange(list_total) == full_list, CAP, live_counts)
    live_mask = jnp.arange(CAP)[None, :] < live_counts[:, None]
    chosen = jnp.where(live_mask, orders, -1)
    return chosen.reshape(FF // BLK, N_GY * CAP).astype(jnp.int32)


def draw_gate_slots(key, part):
    key = jax.random.fold_in(key, 11)
    return slot_lists(key)


def draw_up_slots(key, part):
    key = jax.random.fold_in(key, 12)
    return slot_lists(key)


def draw_down_slots(key, part):
    key = jax.random.fold_in(key, 13)
    return slot_lists(key)


def block_scale(rng, dims, cuts, low, high):
    gain = 1.0
    for axis_at, blocks in cuts:
        steps = jax.random.uniform(jax.random.fold_in(jax.random.fold_in(rng, 6), axis_at), (blocks,), jnp.float32, low / len(cuts), high / len(cuts))
        gain = gain * jnp.repeat(jnp.exp(steps), dims[axis_at] // blocks).reshape((-1,) + (1,) * (len(dims) - 1 - axis_at))
    return gain


def normal_values(key, shape, width, reach, cuts=(), kind=jnp.bfloat16):
    loudness = block_scale(key, shape, cuts, -0.22, 0.18) if cuts else 1.0
    drawn = jax.random.normal(key, shape, jnp.float32) * width * loudness
    return jnp.minimum(jnp.maximum(drawn, -reach), reach).astype(kind)


def setup_inputs(seed: int = 0, part: int = 0) -> dict:
    key_list = jax.random.split(jax.random.key(seed), 8)
    part_splits = jax.random.split(jax.random.fold_in(key_list[7], part), 8)
    activations = normal_values(part_splits[0], (N_GY, TOKENS, D // N_GY), 1.0, 6.0, ((0, 2), (2, 8)))
    gate_tiles = normal_values(key_list[1], (FF // BLK, N_GY * CAP, BLK, BLK), (CAP * N_GY * BLK * 4 // 5) ** -0.5, 0.09375, ((0, 8), (1, 2)))
    up_tiles = normal_values(key_list[2], (FF // BLK, N_GY * CAP, BLK, BLK), (CAP * N_GY * BLK * 4 // 5) ** -0.5, 0.09375, ((0, 8), (1, 2)))
    down_tiles = normal_values(key_list[3], (FF // BLK, N_GY * CAP, BLK, BLK), (FF * (4 * CAP // 5) * N_GY * BLK // D) ** -0.5, 0.046875, ((0, 8), (1, 2)))
    gate_slots = draw_gate_slots(jax.random.fold_in(key_list[7], 71), part)
    up_slots = draw_up_slots(jax.random.fold_in(key_list[7], 71), part)
    down_slots = draw_down_slots(jax.random.fold_in(key_list[7], 71), part)
    return dict(activations=activations, gate_tiles=gate_tiles, up_tiles=up_tiles, down_tiles=down_tiles, gate_slots=gate_slots, up_slots=up_slots, down_slots=down_slots)


def reference(activations, gate_tiles, up_tiles, down_tiles, gate_slots, up_slots, down_slots):
    blocks_half = D // BLK // N_GY
    slot_total = N_GY * CAP
    half_index = (jnp.arange(slot_total) // CAP).astype(jnp.int32)
    whole = jnp.transpose(activations, (1, 0, 2)).reshape(TOKENS, D)
    blocked = whole.reshape(TOKENS, D // BLK, BLK).astype(jnp.float32)

    def project(tile_set, slot_ids):
        block_index = jnp.where(slot_ids >= 0, half_index * blocks_half + slot_ids, 0).astype(jnp.int32)
        keep_flags = (slot_ids >= 0).astype(jnp.float32)
        chosen = blocked[:, block_index, :] * keep_flags[None, :, None]
        return jnp.einsum("tsk,skn->tn", chosen, tile_set.astype(jnp.float32))

    def column(pieces):
        gate_set, up_set, gate_ids, up_ids = pieces
        gate_full = project(gate_set, gate_ids)
        up_full = project(up_set, up_ids)
        return (jax.nn.silu(gate_full) * up_full).astype(jnp.bfloat16)

    hidden = lax.map(column, (gate_tiles, up_tiles, gate_slots, up_slots))

    def spread(running, pieces):
        hidden_block, down_set, down_ids = pieces
        block_index = jnp.where(down_ids >= 0, half_index * blocks_half + down_ids, 0).astype(jnp.int32)
        keep_flags = (down_ids >= 0).astype(jnp.float32)
        contribs = jnp.einsum("tk,skn->tsn", hidden_block.astype(jnp.float32), down_set.astype(jnp.float32))
        contribs = contribs * keep_flags[None, :, None]
        return running.at[:, block_index, :].add(contribs), None

    running = jnp.zeros((TOKENS, D // BLK, BLK), jnp.float32)
    running, _ = lax.scan(spread, running, (hidden, down_tiles, down_slots))
    result = running.reshape(TOKENS, N_GY, D // N_GY)
    return jnp.transpose(result, (1, 0, 2)).astype(jnp.bfloat16)
```

```python
import functools

import jax
import jax.numpy as jnp
from jax import lax
from jax.experimental import pallas as pl
from jax.experimental.pallas import tpu as pltpu
from jax.sharding import PartitionSpec as P

MESH = pl.DeviceIdType.MESH
LINE = 4
GROUP = 4
RING = 4
DOWN_PARTS = 4


def mask_tiles(tile_set, slot_ids):
    return tile_set * (slot_ids >= 0).astype(tile_set.dtype)[:, :, None, None]


def project_dense(row_piece, tile_set, slot_ids):
    row_count = row_piece.shape[0]
    col_blocks, slot_count, tile_size, _ = tile_set.shape
    blocked = row_piece.reshape(row_count, -1, tile_size)
    chosen = jnp.take(blocked, jnp.maximum(slot_ids, 0).reshape(-1), axis=1)
    chosen = chosen.reshape(row_count, col_blocks, slot_count, tile_size)
    result = jnp.einsum("pfsk,fskn->pfn", chosen, tile_set, preferred_element_type=jnp.float32)
    return result.reshape(row_count, col_blocks * tile_size)


def spread_dense(hidden, tile_set, slot_ids, blocks):
    col_blocks, slot_count, tile_size, _ = tile_set.shape
    placing = (slot_ids[:, :, None] == jnp.arange(blocks)[None, None, :]).astype(jnp.bfloat16)
    placed = jnp.einsum("fsd,fskn->fkdn", placing, tile_set, preferred_element_type=jnp.float32)
    weight_block = placed.astype(jnp.bfloat16).reshape(col_blocks * tile_size, blocks * tile_size)
    return jnp.dot(hidden, weight_block, preferred_element_type=jnp.float32)


def general_body(activations, gate_tiles, up_tiles, down_tiles, gate_slots, up_slots, down_slots):
    members = lax.axis_size("gx")
    _, total_rows, column_count = activations.shape
    half_width = column_count * members
    blocks = half_width // gate_tiles.shape[2]
    gate_keep = mask_tiles(gate_tiles, gate_slots)
    up_keep = mask_tiles(up_tiles, up_slots)
    gathered = lax.all_gather(activations, "gx", axis=2, tiled=True)
    row_piece = gathered[0]
    gate_half = project_dense(row_piece, gate_keep, gate_slots)
    up_half = project_dense(row_piece, up_keep, up_slots)
    gate_full, up_full = lax.psum((gate_half, up_half), "gy")
    hidden = (jax.nn.silu(gate_full) * up_full).astype(jnp.bfloat16)
    partial_value = spread_dense(hidden, down_tiles, down_slots, blocks).reshape(
        total_rows, members, column_count
    )
    arrived = lax.all_to_all(partial_value, "gx", split_axis=1, concat_axis=1, tiled=True)
    mixed_out = jnp.sum(arrived, axis=1)
    return mixed_out.astype(jnp.bfloat16)[None, :, :]


def dot(a, b):
    return jnp.dot(a, b, preferred_element_type=jnp.float32)


def kernel(
    gate_ids, up_ids, down_at, x_ref, gate_hbm, up_hbm, down_hbm, out_ref,
    xg, wbuf, dbuf, sums, pair_out, pair_in, hid, yacc,
    far_out, far_in, line_out, above_in, below_in,
    wsem, dsem, pair_ssem, pair_rsem,
    ag_xs, ag_xr, ag_us, ag_ds, ag_zr,
    rs_xs, rs_xr, rs_zs, rs_ur, rs_dr,
):
    blk = xg.shape[1]
    per = x_ref.shape[2] // blk
    blocks = xg.shape[0] - 1
    col_blocks, slots = gate_hbm.shape[0], gate_hbm.shape[1]
    chunks = col_blocks // GROUP
    tiles = down_hbm.shape[0]
    dpart = tiles // DOWN_PARTS

    me = lax.axis_index("gx")
    z, xx = me // 2, me % 2
    other = 2 * z + 1 - xx
    core = 1 - lax.axis_index("gy")

    def weight_copies(c):
        b = c % RING
        rows = pl.ds(c * GROUP, GROUP)
        return (
            pltpu.make_async_copy(gate_hbm.at[rows], wbuf.at[b, 0], wsem.at[b, 0]),
            pltpu.make_async_copy(up_hbm.at[rows], wbuf.at[b, 1], wsem.at[b, 1]),
        )

    def down_copy(i):
        rows = pl.ds(i * dpart, dpart)
        return pltpu.make_async_copy(down_hbm.at[rows], dbuf.at[rows], dsem.at[i])

    for c in range(min(RING, chunks)):
        for copy in weight_copies(c):
            copy.start()
    for i in range(DOWN_PARTS):
        down_copy(i).start()

    barrier = pltpu.get_barrier_semaphore()
    pl.semaphore_signal(barrier, inc=1, device_id={"gx": other}, device_id_type=MESH)
    pl.semaphore_signal(barrier, inc=1, device_id={"gy": core}, device_id_type=MESH)

    @pl.when(z > 0)
    def _():
        pl.semaphore_signal(barrier, inc=1, device_id={"gx": me - 2}, device_id_type=MESH)

    @pl.when(z < LINE - 1)
    def _():
        pl.semaphore_signal(barrier, inc=1, device_id={"gx": me + 2}, device_id_type=MESH)

    for b in range(per):
        xg[me * per + b] = x_ref[0, :, b * blk : (b + 1) * blk]
    xg[blocks] = jnp.zeros_like(xg[blocks])
    dbuf[tiles] = jnp.zeros_like(dbuf[tiles])

    pl.semaphore_wait(barrier, 2 + (z + LINE - 1) // LINE + (2 * LINE - 2 - z) // LINE)

    def piece(zz, side):
        return xg.at[pl.ds((2 * zz + side) * per, per)]

    def line_copy(zz, send, to):
        return pltpu.make_async_remote_copy(
            src_ref=piece(zz, xx), dst_ref=piece(zz, xx), send_sem=send, recv_sem=ag_zr.at[zz],
            device_id={"gx": to}, device_id_type=MESH,
        )

    def up_copy(s):
        return line_copy(z - s, ag_us.at[s], me + 2)

    def dn_copy(s):
        return line_copy(z + s, ag_ds.at[s], me - 2)

    def side_copy(zz, side):
        return pltpu.make_async_remote_copy(
            src_ref=piece(zz, side), dst_ref=piece(zz, side), send_sem=ag_xs.at[zz], recv_sem=ag_xr.at[zz],
            device_id={"gx": other}, device_id_type=MESH,
        )

    @pl.when(z < LINE - 1)
    def _():
        up_copy(0).start()

    @pl.when(z > 0)
    def _():
        dn_copy(0).start()

    side_copy(z, xx).start()
    for s in range(LINE - 1):
        @pl.when(z - 1 - s >= 0)
        def _():
            line_copy(z - 1 - s, ag_us.at[s], me - 2).wait_recv()

            @pl.when(z < LINE - 1)
            def _():
                up_copy(s + 1).start()

            side_copy(z - 1 - s, xx).start()

        @pl.when(z + 1 + s < LINE)
        def _():
            line_copy(z + 1 + s, ag_ds.at[s], me + 2).wait_recv()

            @pl.when(z > 0)
            def _():
                dn_copy(s + 1).start()

            side_copy(z + 1 + s, xx).start()

    for zz in range(LINE):
        side_copy(zz, 1 - xx).wait_recv()

    def pair_copy(c):
        return pltpu.make_async_remote_copy(
            src_ref=pair_out.at[c], dst_ref=pair_in.at[c], send_sem=pair_ssem.at[c], recv_sem=pair_rsem.at[c],
            device_id={"gy": core}, device_id_type=MESH,
        )

    def project(ids, b, which, j, f):
        total = None
        step = 4
        for s0 in range(0, slots, step):
            n = min(step, slots - s0)
            left = jnp.concatenate([xg[ids[f, s0 + i]] for i in range(n)], axis=1)
            right = wbuf[b, which, j, s0 : s0 + n].reshape(n * blk, blk)
            term = dot(left, right)
            total = term if total is None else total + term
        return total

    def activate(c):
        pair_copy(c).wait_recv()
        for j in range(GROUP):
            cols = slice(j * blk, (j + 1) * blk)
            gate = sums[c, 0, :, cols] + pair_in[c, 0, :, cols].astype(jnp.float32)
            up = sums[c, 1, :, cols] + pair_in[c, 1, :, cols].astype(jnp.float32)
            hid[c, :, cols] = (gate / (1.0 + jnp.exp(-gate)) * up).astype(hid.dtype)

    @pl.loop(0, chunks)
    def _(c):
        b = c % RING
        for copy in weight_copies(c):
            copy.wait()
        for j in range(GROUP):
            cols = slice(j * blk, (j + 1) * blk)
            f = c * GROUP + j
            for which, ids in enumerate((gate_ids, up_ids)):
                value = project(ids, b, which, j, f)
                sums[c, which, :, cols] = value
                pair_out[c, which, :, cols] = value.astype(pair_out.dtype)
        pair_copy(c).start()

        @pl.when(c + RING < chunks)
        def _():
            for copy in weight_copies(c + RING):
                copy.start()

        @pl.when(c > 0)
        def _():
            activate(c - 1)

    for i in range(DOWN_PARTS):
        down_copy(i).wait()
    activate(chunks - 1)

    def spread(dest):
        for h in range(per // 2):
            r = dest * per + 2 * h

            def step(g, acc):
                rows = []
                for i in range(GROUP):
                    f = g * GROUP + i
                    rows.append(jnp.concatenate([dbuf[down_at[f, r]], dbuf[down_at[f, r + 1]]], axis=1))
                return acc + dot(hid[g], jnp.concatenate(rows, axis=0))

            yacc[:, 2 * h * blk : 2 * (h + 1) * blk] = lax.fori_loop(
                0, chunks, step, jnp.zeros((xg.shape[1], 2 * blk), jnp.float32)
            )

    order = (3 * (1 - z // 2), (2 + 3 * z) % 5, 1 + z % 2, z)

    def far_copy(zz):
        return pltpu.make_async_remote_copy(
            src_ref=far_out.at[zz], dst_ref=far_in.at[zz], send_sem=rs_xs.at[zz], recv_sem=rs_xr.at[zz],
            device_id={"gx": other}, device_id_type=MESH,
        )

    def rise_copy(zz):
        return pltpu.make_async_remote_copy(
            src_ref=line_out.at[zz], dst_ref=below_in.at[zz], send_sem=rs_zs.at[zz], recv_sem=rs_ur.at[zz],
            device_id={"gx": me + 2}, device_id_type=MESH,
        )

    def fall_copy(zz):
        return pltpu.make_async_remote_copy(
            src_ref=line_out.at[zz], dst_ref=above_in.at[zz], send_sem=rs_zs.at[zz], recv_sem=rs_dr.at[zz],
            device_id={"gx": me - 2}, device_id_type=MESH,
        )

    for k in range(LINE):
        zz = order[k]
        spread(2 * zz + 1 - xx)
        far_out[zz] = yacc[...].astype(far_out.dtype)
        far_copy(zz).start()

    for k in range(LINE):
        zz = order[k]
        spread(2 * zz + xx)
        far_copy(zz).wait_recv()
        yacc[...] += far_in[zz].astype(jnp.float32)

        @pl.when((zz >= z) & (z > 0))
        def _():
            rise_copy(zz).wait_recv()
            yacc[...] += below_in[zz].astype(jnp.float32)

        @pl.when((zz <= z) & (z < LINE - 1))
        def _():
            fall_copy(zz).wait_recv()
            yacc[...] += above_in[zz].astype(jnp.float32)

        if k < LINE - 1:
            line_out[zz] = yacc[...].astype(line_out.dtype)

            @pl.when(zz > z)
            def _():
                rise_copy(zz).start()

            @pl.when(zz < z)
            def _():
                fall_copy(zz).start()

    out_ref[0] = yacc[...].astype(out_ref.dtype)

    for c in range(chunks):
        pair_copy(c).wait_send()
    for zz in range(LINE):
        side_copy(zz, xx).wait_send()
        far_copy(zz).wait_send()
    for s in range(LINE):
        @pl.when((z < LINE - 1) & (z - s >= 0))
        def _():
            up_copy(s).wait_send()

        @pl.when((z > 0) & (z + s < LINE))
        def _():
            dn_copy(s).wait_send()
    for k in range(LINE - 1):
        rise_copy(order[k]).wait_send()


def line_body(activations, gate_tiles, up_tiles, down_tiles, gate_slots, up_slots, down_slots):
    members = lax.axis_size("gx")
    _, rows, columns = activations.shape
    col_blocks, slots, blk, _ = gate_tiles.shape
    blocks = columns * members // blk
    tiles = col_blocks * slots
    chunks = col_blocks // GROUP
    gate_ids = jnp.where(gate_slots < 0, blocks, gate_slots)
    up_ids = jnp.where(up_slots < 0, blocks, up_slots)
    index = jnp.arange(tiles, dtype=jnp.int32).reshape(col_blocks, slots, 1) - tiles
    match = down_slots[:, :, None] == jnp.arange(blocks, dtype=jnp.int32)[None, None, :]
    down_at = tiles + jnp.sum(jnp.where(match, index, 0), axis=1)
    bf16, f32 = jnp.bfloat16, jnp.float32
    dma = pltpu.SemaphoreType.DMA
    smem = pl.BlockSpec(memory_space=pltpu.SMEM)
    vmem = pl.BlockSpec(memory_space=pltpu.VMEM)
    hbm = pl.BlockSpec(memory_space=pltpu.HBM)
    block = (LINE, rows, columns)
    return pl.pallas_call(
        kernel,
        out_shape=jax.ShapeDtypeStruct(activations.shape, bf16),
        in_specs=[smem, smem, smem, vmem, hbm, hbm, hbm],
        out_specs=vmem,
        scratch_shapes=[
            pltpu.VMEM((blocks + 1, rows, blk), bf16),
            pltpu.VMEM((RING, 2, GROUP, slots, blk, blk), bf16),
            pltpu.VMEM((tiles + 1, blk, blk), bf16),
            pltpu.VMEM((chunks, 2, rows, GROUP * blk), f32),
            pltpu.VMEM((chunks, 2, rows, GROUP * blk), bf16),
            pltpu.VMEM((chunks, 2, rows, GROUP * blk), bf16),
            pltpu.VMEM((chunks, rows, GROUP * blk), bf16),
            pltpu.VMEM((rows, columns), f32),
            pltpu.VMEM(block, bf16),
            pltpu.VMEM(block, bf16),
            pltpu.VMEM(block, bf16),
            pltpu.VMEM(block, bf16),
            pltpu.VMEM(block, bf16),
            dma((RING, 2)),
            dma((DOWN_PARTS,)),
            dma((chunks,)),
            dma((chunks,)),
        ] + [dma((LINE,))] * 10,
        compiler_params=pltpu.CompilerParams(
            collective_id=0, has_side_effects=True, vmem_limit_bytes=62 * 1024 * 1024
        ),
        cost_estimate=pl.CostEstimate(
            flops=8 * rows * tiles * blk * blk, bytes_accessed=6 * tiles * blk * blk, transcendentals=0
        ),
    )(gate_ids, up_ids, down_at, activations, gate_tiles, up_tiles, down_tiles.reshape(tiles, blk, blk))


def solution(mesh):
    placed = (
        P("gy", "groups", "gx"),
        P("gx", "gy", None, None),
        P("gx", "gy", None, None),
        P("gx", "gy", None, None),
        P("gx", "gy"),
        P("gx", "gy"),
        P("gx", "gy"),
    )

    def body(*args):
        small = mesh.shape["gx"] == 2 * LINE and mesh.shape["gy"] == 2
        _, rows, columns = args[0].shape
        col_blocks, _, blk, _ = args[1].shape
        fits = rows == blk and columns % (2 * blk) == 0 and col_blocks % GROUP == 0 and blk == 128
        return line_body(*args) if small and fits else general_body(*args)

    return jax.shard_map(
        body, mesh=mesh, in_specs=placed, out_specs=P("gy", "groups", "gx"), check_vma=False
    )
```

```python
import functools

import jax
import jax.numpy as jnp
from jax import lax
from jax.experimental import pallas as pl
from jax.experimental.pallas import tpu as pltpu
from jax.sharding import PartitionSpec as P

MESH = pl.DeviceIdType.MESH
LINE = 4
GROUP = 4
RING = 4
DOWN_PARTS = 4


def mask_tiles(tile_set, slot_ids):
    return tile_set * (slot_ids >= 0).astype(tile_set.dtype)[:, :, None, None]


def project_dense(row_piece, tile_set, slot_ids):
    row_count = row_piece.shape[0]
    col_blocks, slot_count, tile_size, _ = tile_set.shape
    blocked = row_piece.reshape(row_count, -1, tile_size)
    chosen = jnp.take(blocked, jnp.maximum(slot_ids, 0).reshape(-1), axis=1)
    chosen = chosen.reshape(row_count, col_blocks, slot_count, tile_size)
    result = jnp.einsum("pfsk,fskn->pfn", chosen, tile_set, preferred_element_type=jnp.float32)
    return result.reshape(row_count, col_blocks * tile_size)


def spread_dense(hidden, tile_set, slot_ids, blocks):
    col_blocks, slot_count, tile_size, _ = tile_set.shape
    placing = (slot_ids[:, :, None] == jnp.arange(blocks)[None, None, :]).astype(jnp.bfloat16)
    placed = jnp.einsum("fsd,fskn->fkdn", placing, tile_set, preferred_element_type=jnp.float32)
    weight_block = placed.astype(jnp.bfloat16).reshape(col_blocks * tile_size, blocks * tile_size)
    return jnp.dot(hidden, weight_block, preferred_element_type=jnp.float32)


def general_body(activations, gate_tiles, up_tiles, down_tiles, gate_slots, up_slots, down_slots):
    members = lax.axis_size("gx")
    _, total_rows, column_count = activations.shape
    half_width = column_count * members
    blocks = half_width // gate_tiles.shape[2]
    gate_keep = mask_tiles(gate_tiles, gate_slots)
    up_keep = mask_tiles(up_tiles, up_slots)
    gathered = lax.all_gather(activations, "gx", axis=2, tiled=True)
    row_piece = gathered[0]
    gate_half = project_dense(row_piece, gate_keep, gate_slots)
    up_half = project_dense(row_piece, up_keep, up_slots)
    gate_full, up_full = lax.psum((gate_half, up_half), "gy")
    hidden = (jax.nn.silu(gate_full) * up_full).astype(jnp.bfloat16)
    partial_value = spread_dense(hidden, down_tiles, down_slots, blocks).reshape(
        total_rows, members, column_count
    )
    arrived = lax.all_to_all(partial_value, "gx", split_axis=1, concat_axis=1, tiled=True)
    mixed_out = jnp.sum(arrived, axis=1)
    return mixed_out.astype(jnp.bfloat16)[None, :, :]


def dot(a, b):
    return jnp.dot(a, b, preferred_element_type=jnp.float32)


def kernel(
    gate_ids, up_ids, down_at, x_ref, gate_hbm, up_hbm, down_hbm, out_ref,
    xg, wbuf, dbuf, sums, pair_out, pair_in, hid, yacc,
    far_out, far_in, line_out, above_in, below_in,
    wsem, dsem, pair_ssem, pair_rsem,
    ag_xs, ag_xr, ag_us, ag_ds, ag_zr,
    rs_xs, rs_xr, rs_zs, rs_ur, rs_dr,
):
    blk = xg.shape[1]
    per = x_ref.shape[2] // blk
    blocks = xg.shape[0] - 1
    col_blocks, slots = gate_hbm.shape[0], gate_hbm.shape[1]
    chunks = col_blocks // GROUP
    tiles = down_hbm.shape[0]
    dpart = tiles // DOWN_PARTS

    me = lax.axis_index("gx")
    z, xx = me // 2, me % 2
    other = 2 * z + 1 - xx
    core = 1 - lax.axis_index("gy")

    def weight_copies(c):
        b = c % RING
        rows = pl.ds(c * GROUP, GROUP)
        return (
            pltpu.make_async_copy(gate_hbm.at[rows], wbuf.at[b, 0], wsem.at[b, 0]),
            pltpu.make_async_copy(up_hbm.at[rows], wbuf.at[b, 1], wsem.at[b, 1]),
        )

    def down_copy(i):
        rows = pl.ds(i * dpart, dpart)
        return pltpu.make_async_copy(down_hbm.at[rows], dbuf.at[rows], dsem.at[i])

    for c in range(min(RING, chunks)):
        for copy in weight_copies(c):
            copy.start()
    for i in range(DOWN_PARTS):
        down_copy(i).start()

    barrier = pltpu.get_barrier_semaphore()
    pl.semaphore_signal(barrier, inc=1, device_id={"gx": other}, device_id_type=MESH)
    pl.semaphore_signal(barrier, inc=1, device_id={"gy": core}, device_id_type=MESH)

    @pl.when(z > 0)
    def _():
        pl.semaphore_signal(barrier, inc=1, device_id={"gx": me - 2}, device_id_type=MESH)

    @pl.when(z < LINE - 1)
    def _():
        pl.semaphore_signal(barrier, inc=1, device_id={"gx": me + 2}, device_id_type=MESH)

    for b in range(per):
        xg[me * per + b] = x_ref[0, :, b * blk : (b + 1) * blk]
    xg[blocks] = jnp.zeros_like(xg[blocks])
    dbuf[tiles] = jnp.zeros_like(dbuf[tiles])

    pl.semaphore_wait(barrier, 2 + (z + LINE - 1) // LINE + (2 * LINE - 2 - z) // LINE)

    def piece(zz, side):
        return xg.at[pl.ds((2 * zz + side) * per, per)]

    def line_copy(zz, send, to):
        return pltpu.make_async_remote_copy(
            src_ref=piece(zz, xx), dst_ref=piece(zz, xx), send_sem=send, recv_sem=ag_zr.at[zz],
            device_id={"gx": to}, device_id_type=MESH,
        )

    def up_copy(s):
        return line_copy(z - s, ag_us.at[s], me + 2)

    def dn_copy(s):
        return line_copy(z + s, ag_ds.at[s], me - 2)

    def side_copy(zz, side):
        return pltpu.make_async_remote_copy(
            src_ref=piece(zz, side), dst_ref=piece(zz, side), send_sem=ag_xs.at[zz], recv_sem=ag_xr.at[zz],
            device_id={"gx": other}, device_id_type=MESH,
        )

    @pl.when(z < LINE - 1)
    def _():
        up_copy(0).start()

    @pl.when(z > 0)
    def _():
        dn_copy(0).start()

    side_copy(z, xx).start()
    for s in range(LINE - 1):
        @pl.when(z - 1 - s >= 0)
        def _():
            line_copy(z - 1 - s, ag_us.at[s], me - 2).wait_recv()

            @pl.when(z < LINE - 1)
            def _():
                up_copy(s + 1).start()

            side_copy(z - 1 - s, xx).start()

        @pl.when(z + 1 + s < LINE)
        def _():
            line_copy(z + 1 + s, ag_ds.at[s], me + 2).wait_recv()

            @pl.when(z > 0)
            def _():
                dn_copy(s + 1).start()

            side_copy(z + 1 + s, xx).start()

    for zz in range(LINE):
        side_copy(zz, 1 - xx).wait_recv()

    def pair_copy(c):
        return pltpu.make_async_remote_copy(
            src_ref=pair_out.at[c], dst_ref=pair_in.at[c], send_sem=pair_ssem.at[c], recv_sem=pair_rsem.at[c],
            device_id={"gy": core}, device_id_type=MESH,
        )

    def project(ids, b, which, j, f):
        total = None
        step = 4
        for s0 in range(0, slots, step):
            n = min(step, slots - s0)
            left = jnp.concatenate([xg[ids[f, s0 + i]] for i in range(n)], axis=1)
            right = wbuf[b, which, j, s0 : s0 + n].reshape(n * blk, blk)
            term = dot(left, right)
            total = term if total is None else total + term
        return total

    def activate(c):
        pair_copy(c).wait_recv()
        for j in range(GROUP):
            cols = slice(j * blk, (j + 1) * blk)
            gate = sums[c, 0, :, cols] + pair_in[c, 0, :, cols].astype(jnp.float32)
            up = sums[c, 1, :, cols] + pair_in[c, 1, :, cols].astype(jnp.float32)
            hid[c, :, cols] = (gate / (1.0 + jnp.exp(-gate)) * up).astype(hid.dtype)

    @pl.loop(0, chunks)
    def _(c):
        b = c % RING
        for copy in weight_copies(c):
            copy.wait()
        for j in range(GROUP):
            cols = slice(j * blk, (j + 1) * blk)
            f = c * GROUP + j
            for which, ids in enumerate((gate_ids, up_ids)):
                value = project(ids, b, which, j, f)
                sums[c, which, :, cols] = value
                pair_out[c, which, :, cols] = value.astype(pair_out.dtype)
        pair_copy(c).start()

        @pl.when(c + RING < chunks)
        def _():
            for copy in weight_copies(c + RING):
                copy.start()

        @pl.when(c > 0)
        def _():
            activate(c - 1)

    for i in range(DOWN_PARTS):
        down_copy(i).wait()
    activate(chunks - 1)

    def spread(dest):
        for h in range(per // 2):
            r = dest * per + 2 * h

            def step(g, acc):
                rows = []
                for i in range(GROUP):
                    f = g * GROUP + i
                    rows.append(jnp.concatenate([dbuf[down_at[f, r]], dbuf[down_at[f, r + 1]]], axis=1))
                return acc + dot(hid[g], jnp.concatenate(rows, axis=0))

            yacc[:, 2 * h * blk : 2 * (h + 1) * blk] = lax.fori_loop(
                0, chunks, step, jnp.zeros((xg.shape[1], 2 * blk), jnp.float32), unroll=4
            )

    order = (3 * (1 - z // 2), (2 + 3 * z) % 5, 1 + z % 2, z)

    def far_copy(zz):
        return pltpu.make_async_remote_copy(
            src_ref=far_out.at[zz], dst_ref=far_in.at[zz], send_sem=rs_xs.at[zz], recv_sem=rs_xr.at[zz],
            device_id={"gx": other}, device_id_type=MESH,
        )

    def rise_copy(zz):
        return pltpu.make_async_remote_copy(
            src_ref=line_out.at[zz], dst_ref=below_in.at[zz], send_sem=rs_zs.at[zz], recv_sem=rs_ur.at[zz],
            device_id={"gx": me + 2}, device_id_type=MESH,
        )

    def fall_copy(zz):
        return pltpu.make_async_remote_copy(
            src_ref=line_out.at[zz], dst_ref=above_in.at[zz], send_sem=rs_zs.at[zz], recv_sem=rs_dr.at[zz],
            device_id={"gx": me - 2}, device_id_type=MESH,
        )

    for k in range(LINE):
        zz = order[k]
        spread(2 * zz + 1 - xx)
        far_out[zz] = yacc[...].astype(far_out.dtype)
        far_copy(zz).start()

    for k in range(LINE):
        zz = order[k]
        spread(2 * zz + xx)
        far_copy(zz).wait_recv()
        yacc[...] += far_in[zz].astype(jnp.float32)

        @pl.when((zz >= z) & (z > 0))
        def _():
            rise_copy(zz).wait_recv()
            yacc[...] += below_in[zz].astype(jnp.float32)

        @pl.when((zz <= z) & (z < LINE - 1))
        def _():
            fall_copy(zz).wait_recv()
            yacc[...] += above_in[zz].astype(jnp.float32)

        if k < LINE - 1:
            line_out[zz] = yacc[...].astype(line_out.dtype)

            @pl.when(zz > z)
            def _():
                rise_copy(zz).start()

            @pl.when(zz < z)
            def _():
                fall_copy(zz).start()

    out_ref[0] = yacc[...].astype(out_ref.dtype)

    for c in range(chunks):
        pair_copy(c).wait_send()
    for zz in range(LINE):
        side_copy(zz, xx).wait_send()
        far_copy(zz).wait_send()
    for s in range(LINE):
        @pl.when((z < LINE - 1) & (z - s >= 0))
        def _():
            up_copy(s).wait_send()

        @pl.when((z > 0) & (z + s < LINE))
        def _():
            dn_copy(s).wait_send()
    for k in range(LINE - 1):
        rise_copy(order[k]).wait_send()


def line_body(activations, gate_tiles, up_tiles, down_tiles, gate_slots, up_slots, down_slots):
    members = lax.axis_size("gx")
    _, rows, columns = activations.shape
    col_blocks, slots, blk, _ = gate_tiles.shape
    blocks = columns * members // blk
    tiles = col_blocks * slots
    chunks = col_blocks // GROUP
    gate_ids = jnp.where(gate_slots < 0, blocks, gate_slots)
    up_ids = jnp.where(up_slots < 0, blocks, up_slots)
    index = jnp.arange(tiles, dtype=jnp.int32).reshape(col_blocks, slots, 1) - tiles
    match = down_slots[:, :, None] == jnp.arange(blocks, dtype=jnp.int32)[None, None, :]
    down_at = tiles + jnp.sum(jnp.where(match, index, 0), axis=1)
    bf16, f32 = jnp.bfloat16, jnp.float32
    dma = pltpu.SemaphoreType.DMA
    smem = pl.BlockSpec(memory_space=pltpu.SMEM)
    vmem = pl.BlockSpec(memory_space=pltpu.VMEM)
    hbm = pl.BlockSpec(memory_space=pltpu.HBM)
    block = (LINE, rows, columns)
    return pl.pallas_call(
        kernel,
        out_shape=jax.ShapeDtypeStruct(activations.shape, bf16),
        in_specs=[smem, smem, smem, vmem, hbm, hbm, hbm],
        out_specs=vmem,
        scratch_shapes=[
            pltpu.VMEM((blocks + 1, rows, blk), bf16),
            pltpu.VMEM((RING, 2, GROUP, slots, blk, blk), bf16),
            pltpu.VMEM((tiles + 1, blk, blk), bf16),
            pltpu.VMEM((chunks, 2, rows, GROUP * blk), f32),
            pltpu.VMEM((chunks, 2, rows, GROUP * blk), bf16),
            pltpu.VMEM((chunks, 2, rows, GROUP * blk), bf16),
            pltpu.VMEM((chunks, rows, GROUP * blk), bf16),
            pltpu.VMEM((rows, columns), f32),
            pltpu.VMEM(block, bf16),
            pltpu.VMEM(block, bf16),
            pltpu.VMEM(block, bf16),
            pltpu.VMEM(block, bf16),
            pltpu.VMEM(block, bf16),
            dma((RING, 2)),
            dma((DOWN_PARTS,)),
            dma((chunks,)),
            dma((chunks,)),
        ] + [dma((LINE,))] * 10,
        compiler_params=pltpu.CompilerParams(
            collective_id=0, has_side_effects=True, vmem_limit_bytes=62 * 1024 * 1024
        ),
        cost_estimate=pl.CostEstimate(
            flops=8 * rows * tiles * blk * blk, bytes_accessed=6 * tiles * blk * blk, transcendentals=0
        ),
    )(gate_ids, up_ids, down_at, activations, gate_tiles, up_tiles, down_tiles.reshape(tiles, blk, blk))


def solution(mesh):
    placed = (
        P("gy", "groups", "gx"),
        P("gx", "gy", None, None),
        P("gx", "gy", None, None),
        P("gx", "gy", None, None),
        P("gx", "gy"),
        P("gx", "gy"),
        P("gx", "gy"),
    )

    def body(*args):
        small = mesh.shape["gx"] == 2 * LINE and mesh.shape["gy"] == 2
        _, rows, columns = args[0].shape
        col_blocks, _, blk, _ = args[1].shape
        fits = rows == blk and columns % (2 * blk) == 0 and col_blocks % GROUP == 0 and blk == 128
        return line_body(*args) if small and fits else general_body(*args)

    return jax.shard_map(
        body, mesh=mesh, in_specs=placed, out_specs=P("gy", "groups", "gx"), check_vma=False
    )
```

```python
import functools

import jax
import jax.numpy as jnp
from jax import lax
from jax.experimental import pallas as pl
from jax.experimental.pallas import tpu as pltpu
from jax.sharding import PartitionSpec as P

MESH = pl.DeviceIdType.MESH
LINE = 4
GROUP = 4
RING = 4
DOWN_PARTS = 4


def mask_tiles(tile_set, slot_ids):
    return tile_set * (slot_ids >= 0).astype(tile_set.dtype)[:, :, None, None]


def project_dense(row_piece, tile_set, slot_ids):
    row_count = row_piece.shape[0]
    col_blocks, slot_count, tile_size, _ = tile_set.shape
    blocked = row_piece.reshape(row_count, -1, tile_size)
    chosen = jnp.take(blocked, jnp.maximum(slot_ids, 0).reshape(-1), axis=1)
    chosen = chosen.reshape(row_count, col_blocks, slot_count, tile_size)
    result = jnp.einsum("pfsk,fskn->pfn", chosen, tile_set, preferred_element_type=jnp.float32)
    return result.reshape(row_count, col_blocks * tile_size)


def spread_dense(hidden, tile_set, slot_ids, blocks):
    col_blocks, slot_count, tile_size, _ = tile_set.shape
    placing = (slot_ids[:, :, None] == jnp.arange(blocks)[None, None, :]).astype(jnp.bfloat16)
    placed = jnp.einsum("fsd,fskn->fkdn", placing, tile_set, preferred_element_type=jnp.float32)
    weight_block = placed.astype(jnp.bfloat16).reshape(col_blocks * tile_size, blocks * tile_size)
    return jnp.dot(hidden, weight_block, preferred_element_type=jnp.float32)


def general_body(activations, gate_tiles, up_tiles, down_tiles, gate_slots, up_slots, down_slots):
    members = lax.axis_size("gx")
    _, total_rows, column_count = activations.shape
    half_width = column_count * members
    blocks = half_width // gate_tiles.shape[2]
    gate_keep = mask_tiles(gate_tiles, gate_slots)
    up_keep = mask_tiles(up_tiles, up_slots)
    gathered = lax.all_gather(activations, "gx", axis=2, tiled=True)
    row_piece = gathered[0]
    gate_half = project_dense(row_piece, gate_keep, gate_slots)
    up_half = project_dense(row_piece, up_keep, up_slots)
    gate_full, up_full = lax.psum((gate_half, up_half), "gy")
    hidden = (jax.nn.silu(gate_full) * up_full).astype(jnp.bfloat16)
    partial_value = spread_dense(hidden, down_tiles, down_slots, blocks).reshape(
        total_rows, members, column_count
    )
    arrived = lax.all_to_all(partial_value, "gx", split_axis=1, concat_axis=1, tiled=True)
    mixed_out = jnp.sum(arrived, axis=1)
    return mixed_out.astype(jnp.bfloat16)[None, :, :]


def dot(a, b):
    return jnp.dot(a, b, preferred_element_type=jnp.float32)


def kernel(
    gate_ids, up_ids, down_at, x_ref, gate_hbm, up_hbm, down_hbm, out_ref,
    xg, wbuf, dbuf, sums, pair_out, pair_in, hid, yacc,
    far_out, far_in, line_out, above_in, below_in,
    wsem, dsem, pair_ssem, pair_rsem,
    ag_xs, ag_xr, ag_us, ag_ds, ag_zr,
    rs_xs, rs_xr, rs_zs, rs_ur, rs_dr,
):
    blk = xg.shape[1]
    per = x_ref.shape[2] // blk
    blocks = xg.shape[0] - 1
    col_blocks, slots = gate_hbm.shape[0], gate_hbm.shape[1]
    chunks = col_blocks // GROUP
    tiles = down_hbm.shape[0]
    dpart = tiles // DOWN_PARTS

    me = lax.axis_index("gx")
    z, xx = me // 2, me % 2
    other = 2 * z + 1 - xx
    core = 1 - lax.axis_index("gy")

    def weight_copies(c):
        b = c % RING
        rows = pl.ds(c * GROUP, GROUP)
        return (
            pltpu.make_async_copy(gate_hbm.at[rows], wbuf.at[b, 0], wsem.at[b, 0]),
            pltpu.make_async_copy(up_hbm.at[rows], wbuf.at[b, 1], wsem.at[b, 1]),
        )

    def down_copy(i):
        rows = pl.ds(i * dpart, dpart)
        return pltpu.make_async_copy(down_hbm.at[rows], dbuf.at[rows], dsem.at[i])

    for c in range(min(RING, chunks)):
        for copy in weight_copies(c):
            copy.start()
    for i in range(DOWN_PARTS):
        down_copy(i).start()

    barrier = pltpu.get_barrier_semaphore()
    pl.semaphore_signal(barrier, inc=1, device_id={"gx": other}, device_id_type=MESH)
    pl.semaphore_signal(barrier, inc=1, device_id={"gy": core}, device_id_type=MESH)

    @pl.when(z > 0)
    def _():
        pl.semaphore_signal(barrier, inc=1, device_id={"gx": me - 2}, device_id_type=MESH)

    @pl.when(z < LINE - 1)
    def _():
        pl.semaphore_signal(barrier, inc=1, device_id={"gx": me + 2}, device_id_type=MESH)

    for b in range(per):
        xg[me * per + b] = x_ref[0, :, b * blk : (b + 1) * blk]
    xg[blocks] = jnp.zeros_like(xg[blocks])
    dbuf[tiles] = jnp.zeros_like(dbuf[tiles])

    pl.semaphore_wait(barrier, 2 + (z + LINE - 1) // LINE + (2 * LINE - 2 - z) // LINE)

    def piece(zz, side):
        return xg.at[pl.ds((2 * zz + side) * per, per)]

    def line_copy(zz, send, to):
        return pltpu.make_async_remote_copy(
            src_ref=piece(zz, xx), dst_ref=piece(zz, xx), send_sem=send, recv_sem=ag_zr.at[zz],
            device_id={"gx": to}, device_id_type=MESH,
        )

    def up_copy(s):
        return line_copy(z - s, ag_us.at[s], me + 2)

    def dn_copy(s):
        return line_copy(z + s, ag_ds.at[s], me - 2)

    def side_copy(zz, side):
        return pltpu.make_async_remote_copy(
            src_ref=piece(zz, side), dst_ref=piece(zz, side), send_sem=ag_xs.at[zz], recv_sem=ag_xr.at[zz],
            device_id={"gx": other}, device_id_type=MESH,
        )

    @pl.when(z < LINE - 1)
    def _():
        up_copy(0).start()

    @pl.when(z > 0)
    def _():
        dn_copy(0).start()

    side_copy(z, xx).start()
    for s in range(LINE - 1):
        @pl.when(z - 1 - s >= 0)
        def _():
            line_copy(z - 1 - s, ag_us.at[s], me - 2).wait_recv()

            @pl.when(z < LINE - 1)
            def _():
                up_copy(s + 1).start()

            side_copy(z - 1 - s, xx).start()

        @pl.when(z + 1 + s < LINE)
        def _():
            line_copy(z + 1 + s, ag_ds.at[s], me + 2).wait_recv()

            @pl.when(z > 0)
            def _():
                dn_copy(s + 1).start()

            side_copy(z + 1 + s, xx).start()

    for zz in range(LINE):
        side_copy(zz, 1 - xx).wait_recv()

    def pair_copy(c):
        return pltpu.make_async_remote_copy(
            src_ref=pair_out.at[c], dst_ref=pair_in.at[c], send_sem=pair_ssem.at[c], recv_sem=pair_rsem.at[c],
            device_id={"gy": core}, device_id_type=MESH,
        )

    def project(ids, b, which, j, f):
        total = None
        step = 4
        for s0 in range(0, slots, step):
            n = min(step, slots - s0)
            left = jnp.concatenate([xg[ids[f, s0 + i]] for i in range(n)], axis=1)
            right = wbuf[b, which, j, s0 : s0 + n].reshape(n * blk, blk)
            term = dot(left, right)
            total = term if total is None else total + term
        return total

    def activate(c):
        pair_copy(c).wait_recv()
        for j in range(GROUP):
            cols = slice(j * blk, (j + 1) * blk)
            gate = sums[c, 0, :, cols] + pair_in[c, 0, :, cols].astype(jnp.float32)
            up = sums[c, 1, :, cols] + pair_in[c, 1, :, cols].astype(jnp.float32)
            hid[c, :, cols] = (gate / (1.0 + jnp.exp(-gate)) * up).astype(hid.dtype)

    @pl.loop(0, chunks)
    def _(c):
        b = c % RING
        for copy in weight_copies(c):
            copy.wait()
        for j in range(GROUP):
            cols = slice(j * blk, (j + 1) * blk)
            f = c * GROUP + j
            for which, ids in enumerate((gate_ids, up_ids)):
                value = project(ids, b, which, j, f)
                sums[c, which, :, cols] = value
                pair_out[c, which, :, cols] = value.astype(pair_out.dtype)
        pair_copy(c).start()

        @pl.when(c + RING < chunks)
        def _():
            for copy in weight_copies(c + RING):
                copy.start()

        @pl.when(c > 0)
        def _():
            activate(c - 1)

    for i in range(DOWN_PARTS):
        down_copy(i).wait()
    activate(chunks - 1)

    def spread(dest):
        for h in range(per // 2):
            r = dest * per + 2 * h

            def step(g, acc):
                rows = []
                for i in range(GROUP):
                    f = g * GROUP + i
                    rows.append(jnp.concatenate([dbuf[down_at[f, r]], dbuf[down_at[f, r + 1]]], axis=1))
                return acc + dot(hid[g], jnp.concatenate(rows, axis=0))

            yacc[:, 2 * h * blk : 2 * (h + 1) * blk] = lax.fori_loop(
                0, chunks, step, jnp.zeros((xg.shape[1], 2 * blk), jnp.float32), unroll=True
            )

    order = (3 * (1 - z // 2), (2 + 3 * z) % 5, 1 + z % 2, z)

    def far_copy(zz):
        return pltpu.make_async_remote_copy(
            src_ref=far_out.at[zz], dst_ref=far_in.at[zz], send_sem=rs_xs.at[zz], recv_sem=rs_xr.at[zz],
            device_id={"gx": other}, device_id_type=MESH,
        )

    def rise_copy(zz):
        return pltpu.make_async_remote_copy(
            src_ref=line_out.at[zz], dst_ref=below_in.at[zz], send_sem=rs_zs.at[zz], recv_sem=rs_ur.at[zz],
            device_id={"gx": me + 2}, device_id_type=MESH,
        )

    def fall_copy(zz):
        return pltpu.make_async_remote_copy(
            src_ref=line_out.at[zz], dst_ref=above_in.at[zz], send_sem=rs_zs.at[zz], recv_sem=rs_dr.at[zz],
            device_id={"gx": me - 2}, device_id_type=MESH,
        )

    for k in range(LINE):
        zz = order[k]
        spread(2 * zz + 1 - xx)
        far_out[zz] = yacc[...].astype(far_out.dtype)
        far_copy(zz).start()

    for k in range(LINE):
        zz = order[k]
        spread(2 * zz + xx)
        far_copy(zz).wait_recv()
        yacc[...] += far_in[zz].astype(jnp.float32)

        @pl.when((zz >= z) & (z > 0))
        def _():
            rise_copy(zz).wait_recv()
            yacc[...] += below_in[zz].astype(jnp.float32)

        @pl.when((zz <= z) & (z < LINE - 1))
        def _():
            fall_copy(zz).wait_recv()
            yacc[...] += above_in[zz].astype(jnp.float32)

        if k < LINE - 1:
            line_out[zz] = yacc[...].astype(line_out.dtype)

            @pl.when(zz > z)
            def _():
                rise_copy(zz).start()

            @pl.when(zz < z)
            def _():
                fall_copy(zz).start()

    out_ref[0] = yacc[...].astype(out_ref.dtype)

    for c in range(chunks):
        pair_copy(c).wait_send()
    for zz in range(LINE):
        side_copy(zz, xx).wait_send()
        far_copy(zz).wait_send()
    for s in range(LINE):
        @pl.when((z < LINE - 1) & (z - s >= 0))
        def _():
            up_copy(s).wait_send()

        @pl.when((z > 0) & (z + s < LINE))
        def _():
            dn_copy(s).wait_send()
    for k in range(LINE - 1):
        rise_copy(order[k]).wait_send()


def line_body(activations, gate_tiles, up_tiles, down_tiles, gate_slots, up_slots, down_slots):
    members = lax.axis_size("gx")
    _, rows, columns = activations.shape
    col_blocks, slots, blk, _ = gate_tiles.shape
    blocks = columns * members // blk
    tiles = col_blocks * slots
    chunks = col_blocks // GROUP
    gate_ids = jnp.where(gate_slots < 0, blocks, gate_slots)
    up_ids = jnp.where(up_slots < 0, blocks, up_slots)
    index = jnp.arange(tiles, dtype=jnp.int32).reshape(col_blocks, slots, 1) - tiles
    match = down_slots[:, :, None] == jnp.arange(blocks, dtype=jnp.int32)[None, None, :]
    down_at = tiles + jnp.sum(jnp.where(match, index, 0), axis=1)
    bf16, f32 = jnp.bfloat16, jnp.float32
    dma = pltpu.SemaphoreType.DMA
    smem = pl.BlockSpec(memory_space=pltpu.SMEM)
    vmem = pl.BlockSpec(memory_space=pltpu.VMEM)
    hbm = pl.BlockSpec(memory_space=pltpu.HBM)
    block = (LINE, rows, columns)
    return pl.pallas_call(
        kernel,
        out_shape=jax.ShapeDtypeStruct(activations.shape, bf16),
        in_specs=[smem, smem, smem, vmem, hbm, hbm, hbm],
        out_specs=vmem,
        scratch_shapes=[
            pltpu.VMEM((blocks + 1, rows, blk), bf16),
            pltpu.VMEM((RING, 2, GROUP, slots, blk, blk), bf16),
            pltpu.VMEM((tiles + 1, blk, blk), bf16),
            pltpu.VMEM((chunks, 2, rows, GROUP * blk), f32),
            pltpu.VMEM((chunks, 2, rows, GROUP * blk), bf16),
            pltpu.VMEM((chunks, 2, rows, GROUP * blk), bf16),
            pltpu.VMEM((chunks, rows, GROUP * blk), bf16),
            pltpu.VMEM((rows, columns), f32),
            pltpu.VMEM(block, bf16),
            pltpu.VMEM(block, bf16),
            pltpu.VMEM(block, bf16),
            pltpu.VMEM(block, bf16),
            pltpu.VMEM(block, bf16),
            dma((RING, 2)),
            dma((DOWN_PARTS,)),
            dma((chunks,)),
            dma((chunks,)),
        ] + [dma((LINE,))] * 10,
        compiler_params=pltpu.CompilerParams(
            collective_id=0, has_side_effects=True, vmem_limit_bytes=62 * 1024 * 1024
        ),
        cost_estimate=pl.CostEstimate(
            flops=8 * rows * tiles * blk * blk, bytes_accessed=6 * tiles * blk * blk, transcendentals=0
        ),
    )(gate_ids, up_ids, down_at, activations, gate_tiles, up_tiles, down_tiles.reshape(tiles, blk, blk))


def solution(mesh):
    placed = (
        P("gy", "groups", "gx"),
        P("gx", "gy", None, None),
        P("gx", "gy", None, None),
        P("gx", "gy", None, None),
        P("gx", "gy"),
        P("gx", "gy"),
        P("gx", "gy"),
    )

    def body(*args):
        small = mesh.shape["gx"] == 2 * LINE and mesh.shape["gy"] == 2
        _, rows, columns = args[0].shape
        col_blocks, _, blk, _ = args[1].shape
        fits = rows == blk and columns % (2 * blk) == 0 and col_blocks % GROUP == 0 and blk == 128
        return line_body(*args) if small and fits else general_body(*args)

    return jax.shard_map(
        body, mesh=mesh, in_specs=placed, out_specs=P("gy", "groups", "gx"), check_vma=False
    )
```
